128 devices in a mesh: space: 16 (over y_lo, z, core), set: 8 (over y_hi, x).
Axes of the slice: x: 4, y: 4 (y_hi: 2, y_lo: 2; y = y_hi * 2 + y_lo), z: 4, core: 2. Of those that a mesh axis runs over, the one named last changes fastest.
Arguments:
- initial: float32 [16, 128, 256, 128], P('set', 'space'), may hold values from -6 to 6
- conductivity: float32 [128, 256, 128], P('space'), may hold values from 0.3 to 1
- weights: float32 [16, 128, 256, 128], P('set', 'space'), may hold values from -6 to 6
- setting_index: int32 [16], P('set'), may hold values from 0 to 63
- track: int32 [64, 4], replicated, may hold values from 0 to 255
- power: int32 [64, 4], replicated, may hold values from 0 to 3
Outputs:
- final_temperature: float32 [16, 128, 256, 128], P('set', 'space')
- conductivity_gradient: float32 [128, 256, 128], P('space', 'set')
The draws below stay inside these ranges and needn't reach their ends.
All inputs are finite; a program needn't handle non-finite values.
Results may differ from the reference program's by a relative error of at most 0.00002.
Values sent between devices are 32-bit elements; how exact they have to be, the bound alone decides.
A program may use at most 128 MiB of HBM per device.

```python
import math
import jax
import jax.numpy as jnp
from jax import lax

NY = 256
NZ = 128
STEPS = 4
LASERS = 64
NPL = 128
SETTINGS = 16


def set_ends(array, rng, smallest, largest):
    longest = array.shape.index(max(array.shape))
    spots = []
    for shift in (0, 1):
        where = [jax.random.randint(jax.random.fold_in(rng, axis), (), 0, length) for axis, length in enumerate(array.shape)]
        where[longest] = (where[longest] + shift) % array.shape[longest]
        spots.append(tuple(where))
    return array.at[spots[0]].set(smallest).at[spots[1]].set(largest)


def strengthened(drawn, stream_key, source, target, shards_of, factor):
    def block_of(position):
        return (jnp.arange(drawn.shape[position]) // (drawn.shape[position] // shards_of)).reshape((-1,) + (1,) * (drawn.ndim - 1 - position))

    first = jax.random.permutation(stream_key, shards_of)[block_of(target)]
    other_side = (block_of(target) + shards_of // 2) % shards_of
    return jnp.where((block_of(source) == first) | (block_of(source) == other_side), factor * drawn, drawn)


def steps_of(own_key, shape, split, least, largest):
    level, own = 1.0, jax.random.fold_in(own_key, 6)
    for position, parts in split:
        steps = jnp.exp(jax.random.uniform(jax.random.fold_in(own, position), (parts,), jnp.float32, least / len(split), largest / len(split)))
        level = level * jnp.repeat(steps, shape[position] // parts).reshape([-1 if axis == position else 1 for axis in range(len(shape))])
    return level


def bell_draw(rng, extent, width, most, cuts=(), held_as=jnp.bfloat16):
    array = jax.random.normal(rng, extent, jnp.float32) * width
    if len(cuts) > 0:
        array = steps_of(rng, extent, cuts, -0.22, 0.18) * array
    return jnp.clip(array, min=-most, max=most).astype(held_as)


def noise_with(key, shape, width, reach, shards, heavy, dtype=jnp.bfloat16):
    array = width * jax.random.normal(key, shape, jnp.float32)
    if shards:
        array = array * steps_of(key, shape, shards, -0.22, 0.18)
    return jnp.clip(strengthened(array, jax.random.fold_in(key, 3), *heavy), -reach, reach).astype(dtype)


def setup_inputs(seed: int = 0) -> dict:
    keys = jax.random.split(jax.random.key(seed), 7)
    initial = bell_draw(keys[0], (SETTINGS, NPL, NY, NZ), 1.0, 6.0, ((0, 8), (1, 16)), jnp.float32)
    conductivity = jnp.clip(jnp.exp(math.log(1.0) - 1.2039728 * jax.random.uniform(keys[1], (NPL, NY, NZ), jnp.float32) ** steps_of(keys[1], (NPL, NY, NZ), ((0, 16),), -0.2, 0.2)), 0.3, 1.0)
    weights = noise_with(keys[2], (SETTINGS, NPL, NY, NZ), 1.0, 6.0, ((0, 8), (1, 16)), (0, 2, 8, 2.0), jnp.float32)
    setting_index = set_ends(jax.random.randint(keys[3], (SETTINGS,), 0, LASERS), jax.random.fold_in(keys[3], 1), 0, LASERS - 1).astype(jnp.int32)
    track = set_ends(jax.random.randint(keys[4], (LASERS, STEPS), 0, NY), jax.random.fold_in(keys[4], 1), 0, NY - 1).astype(jnp.int32)
    power = set_ends(jax.random.randint(keys[5], (LASERS, STEPS), 0, 4), jax.random.fold_in(keys[5], 1), 0, 3).astype(jnp.int32)
    return dict(initial=initial, conductivity=conductivity, weights=weights, setting_index=setting_index, track=track, power=power)


DT = 0.15

def conduct(thermal):
    return 1.0 / (1.0 + thermal * thermal)

def source_field(y_start, power_level):
    y_cells = jnp.arange(NY).astype(jnp.float32)
    z_cells = jnp.arange(NZ).astype(jnp.float32)
    offset = (y_cells - y_start) * 16.0 / NY
    prof_y = jnp.exp(-(offset * offset))
    prof_z = jnp.exp(-4.0 * z_cells / NZ)
    return 0.5 * (1.0 + power_level) * prof_y[:, None] * prof_z[None, :]

def advance(thermal, kappa, heat):
    coeffs = kappa * conduct(thermal)
    padded_temp = jnp.pad(thermal, 1)
    padded_coef = jnp.pad(coeffs, 1)
    slices = [(slice(2, None), slice(1, -1), slice(1, -1)), (slice(0, -2), slice(1, -1), slice(1, -1)), (slice(1, -1), slice(2, None), slice(1, -1)), (slice(1, -1), slice(0, -2), slice(1, -1)), (slice(1, -1), slice(1, -1), slice(2, None)), (slice(1, -1), slice(1, -1), slice(0, -2))]
    flux = jnp.zeros_like(thermal)
    for where in slices:
        flux = flux + 0.5 * (coeffs + padded_coef[where]) * (padded_temp[where] - thermal)
    return thermal + DT * (flux + heat[None])

def reference(initial, conductivity, weights, setting_index, track, power):

    def per_setting(carry, inputs):
        start_temp, weight_row, setting = inputs
        track_row = track[setting]
        power_row = power[setting]

        def forward(kappa):
            thermal = start_temp
            for index_step in range(STEPS):
                heat = source_field(track_row[index_step].astype(jnp.float32), power_row[index_step].astype(jnp.float32))
                thermal = advance(thermal, kappa, heat)
            return thermal
        final, pull_back = jax.vjp(forward, conductivity)
        pulled, = pull_back(weight_row)
        return (carry + pulled, final)
    gradient, finals = lax.scan(per_setting, jnp.zeros(conductivity.shape, jnp.float32), (initial, weights, setting_index))
    return (finals, gradient)
```

```python
import functools

import jax
import jax.numpy as jnp
from jax import lax
from jax.experimental import pallas as pl
from jax.experimental.pallas import tpu as pltpu
from jax.sharding import PartitionSpec as P

STEPS = 4
DT = 0.15
HALF = 0.5 * DT
BLOCKS = 8
LANES = 128
MESH = pl.DeviceIdType.MESH


def recip(value):
    return pl.reciprocal(value, approx=True)


def kernel(planes, inner, set_size, space_size, *refs):
    init_hbm, cond_hbm, weights_hbm, index_smem, track_smem, power_smem, final_hbm, grad_hbm = refs[:8]
    refs = list(refs[8:])

    def take(*shape):
        if not shape:
            return refs.pop(0)
        return [take(*shape[1:]) for _ in range(shape[0])]

    temp = take(STEPS + 1, 2)
    coef = take(STEPS, 2)
    az = take(STEPS, 2)
    dz = take(STEPS, 2)
    lam = take(2, 2)
    hz, hz_low, mz, mz_low = (take(2) for _ in range(4))
    kap, heat, acc, roll_u, roll_a = (take() for _ in range(5))
    share, inbox, inbox_y = (take() for _ in range(3))
    in_sem, out_sem, k_send, k_recv, u_send, u_recv, l_send, l_recv, g_sem, x_send, x_recv, y_send, y_recv = (
        take() for _ in range(13)
    )
    space = lax.axis_index("space")
    own_set = lax.axis_index("set")
    core = lax.rem(space, 2)
    top = core == 1
    edge = (jnp.where(top, planes, 1), jnp.where(top, 1, planes))
    halo = (jnp.where(top, planes + 1, 0), jnp.where(top, 0, planes + 1))
    there = (jnp.where(top, 0, planes + 1), jnp.where(top, planes + 1, 0))
    partner = (
        jnp.clip(jnp.where(top, space + 1, space - 1), 0, space_size - 1),
        jnp.where(top, space - 1, space + 1),
    )
    has_far = jnp.logical_and(space != 0, space != space_size - 1)
    lane = lax.broadcasted_iota(jnp.int32, (BLOCKS, LANES), 1)
    sub = lax.broadcasted_iota(jnp.int32, (BLOCKS, LANES), 0)
    not_last = lane < LANES - 1
    first_lane = lane == 0

    def relayout(src, dst, sem):
        return [
            pltpu.make_async_copy(
                src.at[:, pl.ds(b * inner, inner), :],
                dst.at[pl.ds(1, planes), :, b, :],
                sem.at[b],
            )
            for b in range(BLOCKS)
        ]

    loads = [
        relayout(init_hbm.at[0], temp[0][0], in_sem.at[0]),
        relayout(cond_hbm, kap, in_sem.at[1]),
        relayout(init_hbm.at[1], temp[0][1], in_sem.at[2]),
        relayout(weights_hbm.at[0], lam[0][0], in_sem.at[3]),
        relayout(weights_hbm.at[1], lam[0][1], in_sem.at[4]),
    ]
    for group in loads:
        for copy in group:
            copy.start()

    barrier = pltpu.get_barrier_semaphore()
    pl.semaphore_signal(barrier, inc=1, device_id=(partner[1], own_set), device_id_type=MESH)

    @pl.when(has_far)
    def _():
        pl.semaphore_signal(barrier, inc=1, device_id=(partner[0], own_set), device_id_type=MESH)

    own_y, own_x = own_set // 4, lax.rem(own_set, 4)
    x_right, x_left, x_far = (lax.rem(own_x + i, 4) for i in (1, 3, 2))
    set_right, set_left = own_y * 4 + x_right, own_y * 4 + x_left
    set_y = (1 - own_y) * 4 + own_x
    for other_set in (set_right, set_left, set_y):
        pl.semaphore_signal(barrier, inc=1, device_id=(space, other_set), device_id_type=MESH)

    def swap(ref, side, send, recv):
        return pltpu.make_async_remote_copy(
            src_ref=ref.at[edge[side]],
            dst_ref=ref.at[there[side]],
            send_sem=send,
            recv_sem=recv,
            device_id=(partner[side], own_set),
            device_id_type=MESH,
        )

    def move_temp(side, s, n):
        return swap(temp[n][s], side, u_send.at[side, s, n], u_recv.at[side, s, n])

    def move_lam(side, s, m):
        return swap(lam[m % 2][s], side, l_send.at[side, s, m], l_recv.at[side, s, m])

    def move_kap(side):
        return swap(kap, side, k_send.at[side], k_recv.at[side])

    def each_side(side, do):
        if side:
            do()
        else:
            pl.when(has_far)(do)

    @pl.when(jnp.logical_not(has_far))
    def _():
        zero = jnp.zeros((inner, BLOCKS, LANES), jnp.float32)
        kap[halo[0]] = zero
        for s in range(2):
            for n in range(STEPS):
                temp[n][s][halo[0]] = zero
            for n in range(2):
                lam[n][s][halo[0]] = zero

    prof_z = jnp.exp(-4.0 * lane.astype(jnp.float32) / LANES)

    def make_heat(i, carry):
        s = i // STEPS
        n = lax.rem(i, STEPS)
        row = index_smem[s]
        y0 = track_smem[row, n].astype(jnp.float32)
        level = power_smem[row, n].astype(jnp.float32)
        plane = prof_z * (DT * 0.5 * (1.0 + level))

        def rows(y, c):
            offset = ((sub * inner + y).astype(jnp.float32) - y0) * (16.0 / (inner * BLOCKS))
            heat[i, y] = plane * jnp.exp(-(offset * offset))
            return c

        return lax.fori_loop(0, inner, rows, carry, unroll=8)

    lax.fori_loop(0, 2 * STEPS, make_heat, 0)

    def clear(y, c):
        for p in range(planes):
            acc[p, y] = jnp.zeros((BLOCKS, LANES), jnp.float32)
        return c

    lax.fori_loop(0, inner, clear, 0)

    pl.semaphore_wait(barrier, jnp.where(has_far, 5, 4))

    for which, go in ((0, lambda side: move_temp(side, 0, 0)), (1, move_kap), (2, lambda side: move_temp(side, 1, 0))):
        for copy in loads[which]:
            copy.wait()
        for side in range(2):
            each_side(side, lambda go=go, side=side: go(side).start())

    def scale(p):
        for k in range(inner):
            kap[p, k] = HALF * kap[p, k]

    each_side(0, lambda: move_kap(0).wait_send())
    move_kap(1).wait_send()

    def scale_all(p, c):
        scale(p)
        return c

    lax.fori_loop(1, planes + 1, scale_all, 0)

    def wrapped(value, shift, last):
        return jnp.where(sub == last, 0.0, pltpu.roll(value, shift, 0))

    def before(rows):
        return [wrapped(rows[-1], 1, 0)] + rows[:-1]

    def load(ref, p):
        return [ref[p, k] for k in range(inner)]

    def shifted(value):
        return pltpu.roll(value, LANES - 1, 1)

    def spread_temp(s, n):
        u_ref, a_ref = temp[n][s], coef[n][s]

        def first(p, k):
            roll_u[k] = shifted(u_ref[p, k])
            roll_a[k] = shifted(a_ref[p, k])

        def second(p, k):
            u, a = u_ref[p, k], a_ref[p, k]
            face = a + jnp.where(not_last, roll_a[k], 0.0)
            diff = jnp.where(not_last, roll_u[k], 0.0) - u
            g = face * diff
            az[n][s][p - 1, k] = face
            dz[n][s][p - 1, k] = diff
            hz[s][p - 1, k] = g
            hz_low[s][p - 1, k] = pltpu.roll(g, 1, 1)

        return first, second

    def spread_lam(s, n, whole):
        v_ref = lam[(n + 1) % 2][s]

        def first(p, k):
            roll_u[k] = shifted(v_ref[p, k])

        def second(p, k):
            d = jnp.where(not_last, roll_u[k], 0.0) - v_ref[p, k]
            m = dz[n][s][p - 1, k] * d
            mz[s][p - 1, k] = m
            mz_low[s][p - 1, k] = pltpu.roll(m, 1, 1)
            if whole:
                h = az[n][s][p - 1, k] * d
                hz[s][p - 1, k] = h
                hz_low[s][p - 1, k] = pltpu.roll(h, 1, 1)

        return first, second

    def plane_coef(s, n, p):
        for k in range(inner):
            u = temp[n][s][p, k]
            coef[n][s][p, k] = kap[p, k] * recip(1.0 + u * u)

    def forward(s, n):
        u_ref, a_ref, new = temp[n][s], coef[n][s], temp[n + 1][s]

        def do(p):
            u0, a0 = u_ref[p, 0], a_ref[p, 0]
            ub, ab = wrapped(u_ref[p, inner - 1], 1, 0), wrapped(a_ref[p, inner - 1], 1, 0)
            low = (ab + a0) * (u0 - ub)
            u, a = u0, a0
            for k in range(inner):
                if k + 1 < inner:
                    uy, ay = u_ref[p, k + 1], a_ref[p, k + 1]
                else:
                    uy, ay = wrapped(u0, BLOCKS - 1, BLOCKS - 1), wrapped(a0, BLOCKS - 1, BLOCKS - 1)
                high = (a + ay) * (uy - u)
                flux = (a + a_ref[p + 1, k]) * (u_ref[p + 1, k] - u)
                flux = flux + (a + a_ref[p - 1, k]) * (u_ref[p - 1, k] - u)
                flux = flux + (high - low)
                flux = flux + (hz[s][p - 1, k] - jnp.where(first_lane, a * u, hz_low[s][p - 1, k]))
                later = (u + heat[s * STEPS + n, k]) + flux
                new[p, k] = later
                if n + 1 < STEPS:
                    coef[n + 1][s][p, k] = kap[p, k] * recip(1.0 + later * later)
                low, u, a = high, uy, ay

        return do

    def backward(s, n):
        whole = n > 0
        u_ref, a_ref = temp[n][s], coef[n][s]
        v_ref, new = lam[(n + 1) % 2][s], lam[n % 2][s]

        def do(p):
            def across(ref, k):
                if k < 0:
                    return wrapped(ref[p, inner - 1], 1, 0)
                if k == inner:
                    return wrapped(ref[p, 0], BLOCKS - 1, BLOCKS - 1)
                return ref[p, k]

            u, v = u_ref[p, 0], v_ref[p, 0]
            d = v - across(v_ref, -1)
            m_low = (u - across(u_ref, -1)) * d
            if whole:
                a = a_ref[p, 0]
                h_low = (a + across(a_ref, -1)) * d
            for k in range(inner):
                uy, vy = across(u_ref, k + 1), across(v_ref, k + 1)
                d = vy - v
                d_up, d_down = v_ref[p + 1, k] - v, v_ref[p - 1, k] - v
                m_high = (uy - u) * d
                total = (u_ref[p + 1, k] - u) * d_up + (u_ref[p - 1, k] - u) * d_down
                total = total + (m_high + m_low)
                total = total + (mz[s][p - 1, k] + jnp.where(first_lane, u * v, mz_low[s][p - 1, k]))
                t = total * recip(1.0 + u * u)
                acc[p - 1, k] = acc[p - 1, k] + t
                if whole:
                    ay = across(a_ref, k + 1)
                    h_high = (a + ay) * d
                    flux = (a + a_ref[p + 1, k]) * d_up + (a + a_ref[p - 1, k]) * d_down
                    flux = flux + (h_high - h_low)
                    flux = flux + (hz[s][p - 1, k] - jnp.where(first_lane, a * v, hz_low[s][p - 1, k]))
                    half = (a * u) * t
                    new[p, k] = (v + flux) + (half + half)
                    a, h_low = ay, h_high
                u, v, m_low = uy, vy, m_high

        return do

    def plane_of(t):
        away = jnp.where(top, t, planes + 1 - t)
        return jnp.where(t == 0, edge[0], away)

    def sweep(main, other, at):
        def body(t, c):
            for when, do in at.items():
                pl.when(t == when)(do)
            p = plane_of(t)
            past = plane_of(jnp.maximum(t - 1, 0))

            if other is not None:
                for part, q in ((other[1], past), (other[0], p)):
                    for k in range(inner):
                        part(q, k)
            if main is not None:
                main(p)
            return c

        lax.fori_loop(0, planes, body, 0)
        if other is not None:
            for k in range(inner):
                other[1](plane_of(planes - 1), k)

    def first_coef(p, c):
        for s in range(2):
            plane_coef(s, 0, p)
        return c

    lax.fori_loop(1, planes + 1, first_coef, 0)
    sweep(None, spread_temp(0, 0), {})

    def both_kap(side):
        each_side(side, lambda: move_kap(side).wait_recv())
        scale(halo[side])

    both_kap(1)
    both_kap(0)

    for n in range(STEPS):
        for s in range(2):

            def at_first(s=s, n=n):
                each_side(0, lambda: move_temp(0, s, n).wait_recv())
                plane_coef(s, n, halo[0])

            def at_second(s=s, n=n):
                if n + 1 < STEPS:
                    each_side(0, lambda: move_temp(0, s, n + 1).start())
                move_temp(1, s, n).wait_recv()
                plane_coef(s, n, halo[1])

            at = {0: at_first, 1: at_second}
            if n + 1 < STEPS:
                at[2] = lambda s=s, n=n: move_temp(1, s, n + 1).start()
            if s == 0:
                other = spread_temp(1, n)
            elif n + 1 < STEPS:
                other = spread_temp(0, n + 1)
            else:
                other = spread_lam(0, n, True)
            sweep(forward(s, n), other, at)
        if n == STEPS - 2:
            for s in range(2):
                for copy in loads[3 + s]:
                    copy.wait()
                for side in range(2):
                    each_side(side, lambda: move_lam(side, s, STEPS).start())

    stores = []
    for s in range(2):
        for b in range(BLOCKS):
            copy = pltpu.make_async_copy(
                temp[STEPS][s].at[pl.ds(1, planes), :, b, :],
                final_hbm.at[s, :, pl.ds(b * inner, inner), :],
                out_sem.at[s, b],
            )
            copy.start()
            stores.append(copy)

    for n in reversed(range(STEPS)):
        for s in range(2):

            def at_first(s=s, n=n):
                each_side(0, lambda: move_lam(0, s, n + 1).wait_recv())
                if 0 < n <= STEPS - 2:
                    each_side(0, lambda: move_lam(0, s, n + 2).wait_send())
                    move_lam(1, s, n + 2).wait_send()

            def at_second(s=s, n=n):
                if n > 0:
                    each_side(0, lambda: move_lam(0, s, n).start())
                move_lam(1, s, n + 1).wait_recv()

            at = {0: at_first, 1: at_second}
            if n > 0:
                at[2] = lambda s=s, n=n: move_lam(1, s, n).start()
            if s == 0:
                other = spread_lam(1, n, n > 0)
            elif n > 0:
                other = spread_lam(0, n - 1, n > 1)
            else:
                other = None
            sweep(backward(s, n), other, at)

    half = planes // 2
    shares = [
        pltpu.make_async_copy(acc.at[:, :, b, :], share.at[b // 4, b % 4], g_sem.at[b])
        for b in range(BLOCKS)
    ]
    for copy in shares:
        copy.start()
    for copy in shares:
        copy.wait()

    def along_x(way, slot, column, low):
        return pltpu.make_async_remote_copy(
            src_ref=share.at[:, column, pl.ds(low, half)],
            dst_ref=inbox.at[way, slot],
            send_sem=x_send.at[way, slot],
            recv_sem=x_recv.at[way, slot],
            device_id=(space, set_left if way else set_right),
            device_id_type=MESH,
        )

    column = (x_right, x_left)
    first = (0, half)
    sends = [along_x(way, 0, x_far, first[way]) for way in range(2)]
    sends += [along_x(way, 1, column[way], half - first[way]) for way in range(2)]
    for copy in sends:
        copy.start()

    def add_in(y, column, low, way, slot):
        for p in range(half):
            share[y, column, low + p] = share[y, column, low + p] + inbox[way, slot, y, p]

    for way in range(2):
        sends[way].wait_recv()
        for y in range(2):
            add_in(y, column[way], first[way], way, 0)
        onward = along_x(way, 2, column[way], first[way])
        onward.start()
        sends.append(onward)
    for way in range(2):
        along_x(way, 1, column[way], half - first[way]).wait_recv()
        for y in range(2):
            add_in(y, own_x, half - first[way], way, 1)

    def along_y(way):
        return pltpu.make_async_remote_copy(
            src_ref=share.at[1 - own_y, own_x, pl.ds(first[way], half)],
            dst_ref=inbox_y.at[pl.ds(first[way], half)],
            send_sem=y_send.at[way],
            recv_sem=y_recv.at[way],
            device_id=(space, set_y),
            device_id_type=MESH,
        )

    for way in range(2):
        along_x(way, 2, column[way], first[way]).wait_recv()
        add_in(1 - own_y, own_x, first[way], way, 2)
        along_y(way).start()
        add_in(own_y, own_x, first[way], way, 2)
    for way in range(2):
        along_y(way).wait_recv()
        for p in range(half):
            q = first[way] + p
            inbox_y[q] = -HALF * (share[own_y, own_x, q] + inbox_y[q])
        copy = pltpu.make_async_copy(
            inbox_y.at[pl.ds(first[way], half)], grad_hbm.at[pl.ds(first[way], half)], out_sem.at[2, way]
        )
        copy.start()
        stores.append(copy)
    for copy in sends:
        copy.wait_send()
    for way in range(2):
        along_y(way).wait_send()
    for s in range(2):
        for n in range(STEPS):
            each_side(0, lambda: move_temp(0, s, n).wait_send())
            move_temp(1, s, n).wait_send()
        for m in (1, 2):
            each_side(0, lambda: move_lam(0, s, m).wait_send())
            move_lam(1, s, m).wait_send()
    for copy in stores:
        copy.wait()


def local(set_size, space_size, initial, conductivity, weights, setting_index, track, power):
    settings, planes, y_count, lanes = initial.shape
    inner = y_count // BLOCKS
    tile = (inner, BLOCKS, lanes)
    any_ref = pl.BlockSpec(memory_space=pl.ANY)
    smem = pl.BlockSpec(memory_space=pltpu.SMEM)
    f32 = jnp.float32
    dma = pltpu.SemaphoreType.DMA
    return pl.pallas_call(
        functools.partial(kernel, planes, inner, set_size, space_size),
        out_shape=(
            jax.ShapeDtypeStruct(initial.shape, f32),
            jax.ShapeDtypeStruct((planes, y_count // set_size, lanes), f32),
        ),
        in_specs=[any_ref] * 3 + [smem] * 3,
        out_specs=[any_ref] * 2,
        scratch_shapes=[pltpu.VMEM((planes + 2,) + tile, f32)] * (4 * STEPS + 2)
        + [pltpu.VMEM((planes,) + tile, f32)] * (4 * STEPS)
        + [pltpu.VMEM((planes + 2,) + tile, f32)] * 4
        + [pltpu.VMEM((planes,) + tile, f32)] * 8
        + [
            pltpu.VMEM((planes + 2,) + tile, f32),
            pltpu.VMEM((settings * STEPS,) + tile, f32),
            pltpu.VMEM((planes,) + tile, f32),
            pltpu.VMEM(tile, f32),
            pltpu.VMEM(tile, f32),
            pltpu.VMEM((2, 4, planes, inner, lanes), f32),
            pltpu.VMEM((2, 3, 2, planes // 2, inner, lanes), f32),
            pltpu.VMEM((planes, inner, lanes), f32),
            dma((5, BLOCKS)),
            dma((3, BLOCKS)),
            dma((2,)),
            dma((2,)),
            dma((2, settings, STEPS)),
            dma((2, settings, STEPS)),
            dma((2, settings, STEPS + 1)),
            dma((2, settings, STEPS + 1)),
            dma((BLOCKS,)),
            dma((2, 3)),
            dma((2, 3)),
            dma((2,)),
            dma((2,)),
        ],
        compiler_params=pltpu.CompilerParams(
            collective_id=0, has_side_effects=True, vmem_limit_bytes=62 * 2**20
        ),
    )(initial, conductivity, weights, setting_index, track, power)


def solution(mesh):
    in_specs = (
        P("set", "space", None, None),
        P("space", None, None),
        P("set", "space", None, None),
        P("set"),
        P(),
        P(),
    )
    out_specs = (P("set", "space", None, None), P("space", "set", None))
    return jax.shard_map(
        functools.partial(local, mesh.shape["set"], mesh.shape["space"]),
        mesh=mesh,
        in_specs=in_specs,
        out_specs=out_specs,
        check_vma=False,
    )
```

```python
import functools

import jax
import jax.numpy as jnp
from jax import lax
from jax.experimental import pallas as pl
from jax.experimental.pallas import tpu as pltpu
from jax.sharding import PartitionSpec as P

STEPS = 4
DT = 0.15
HALF = 0.5 * DT
BLOCKS = 8
LANES = 128
MESH = pl.DeviceIdType.MESH


def recip(value):
    return pl.reciprocal(value, approx=True)


def kernel(planes, inner, set_size, space_size, *refs):
    init_hbm, cond_hbm, weights_hbm, index_smem, track_smem, power_smem, final_hbm, grad_hbm = refs[:8]
    refs = list(refs[8:])

    def take(*shape):
        if not shape:
            return refs.pop(0)
        return [take(*shape[1:]) for _ in range(shape[0])]

    temp = take(STEPS + 1, 2)
    coef = take(STEPS, 2)
    az = take(STEPS, 2)
    dz = take(STEPS, 2)
    lam = take(2, 2)
    hz, hz_low, mz, mz_low = (take(2) for _ in range(4))
    kap, heat, acc, roll_u, roll_a = (take() for _ in range(5))
    share, inbox, inbox_y = (take() for _ in range(3))
    in_sem, out_sem, k_send, k_recv, u_send, u_recv, l_send, l_recv, g_sem, x_send, x_recv, y_send, y_recv = (
        take() for _ in range(13)
    )
    space = lax.axis_index("space")
    own_set = lax.axis_index("set")
    core = lax.rem(space, 2)
    top = core == 1
    edge = (jnp.where(top, planes, 1), jnp.where(top, 1, planes))
    halo = (jnp.where(top, planes + 1, 0), jnp.where(top, 0, planes + 1))
    there = (jnp.where(top, 0, planes + 1), jnp.where(top, planes + 1, 0))
    partner = (
        jnp.clip(jnp.where(top, space + 1, space - 1), 0, space_size - 1),
        jnp.where(top, space - 1, space + 1),
    )
    has_far = jnp.logical_and(space != 0, space != space_size - 1)
    lane = lax.broadcasted_iota(jnp.int32, (BLOCKS, LANES), 1)
    sub = lax.broadcasted_iota(jnp.int32, (BLOCKS, LANES), 0)
    not_last = lane < LANES - 1
    first_lane = lane == 0

    def relayout(src, dst, sem):
        return [
            pltpu.make_async_copy(
                src.at[:, pl.ds(b * inner, inner), :],
                dst.at[pl.ds(1, planes), :, b, :],
                sem.at[b],
            )
            for b in range(BLOCKS)
        ]

    loads = [
        relayout(init_hbm.at[0], temp[0][0], in_sem.at[0]),
        relayout(cond_hbm, kap, in_sem.at[1]),
        relayout(init_hbm.at[1], temp[0][1], in_sem.at[2]),
        relayout(weights_hbm.at[0], lam[0][0], in_sem.at[3]),
        relayout(weights_hbm.at[1], lam[0][1], in_sem.at[4]),
    ]
    for group in loads:
        for copy in group:
            copy.start()

    barrier = pltpu.get_barrier_semaphore()
    pl.semaphore_signal(barrier, inc=1, device_id=(partner[1], own_set), device_id_type=MESH)

    @pl.when(has_far)
    def _():
        pl.semaphore_signal(barrier, inc=1, device_id=(partner[0], own_set), device_id_type=MESH)

    own_y, own_x = own_set // 4, lax.rem(own_set, 4)
    x_right, x_left, x_far = (lax.rem(own_x + i, 4) for i in (1, 3, 2))
    set_right, set_left = own_y * 4 + x_right, own_y * 4 + x_left
    set_y = (1 - own_y) * 4 + own_x
    for other_set in (set_right, set_left, set_y):
        pl.semaphore_signal(barrier, inc=1, device_id=(space, other_set), device_id_type=MESH)

    part = inner // 2

    def swap(ref, lane_id, send, recv):
        side = lane_id // 2
        rows = pl.ds(0, inner) if side else pl.ds(lane_id * part, part)
        return pltpu.make_async_remote_copy(
            src_ref=ref.at[edge[side], rows],
            dst_ref=ref.at[there[side], rows],
            send_sem=send,
            recv_sem=recv,
            device_id=(partner[side], own_set),
            device_id_type=MESH,
        )

    def move_temp(i, s, n):
        return swap(temp[n][s], i, u_send.at[i, s, n], u_recv.at[i, s, n])

    def move_lam(i, s, m):
        return swap(lam[m % 2][s], i, l_send.at[i, s, m], l_recv.at[i, s, m])

    def move_kap(i):
        return swap(kap, i, k_send.at[i], k_recv.at[i])

    def each_way(i, do):
        if i == 2:
            do()
        else:
            pl.when(has_far)(do)

    @pl.when(jnp.logical_not(has_far))
    def _():
        zero = jnp.zeros((inner, BLOCKS, LANES), jnp.float32)
        kap[halo[0]] = zero
        for s in range(2):
            for n in range(STEPS):
                temp[n][s][halo[0]] = zero
            for n in range(2):
                lam[n][s][halo[0]] = zero

    prof_z = jnp.exp(-4.0 * lane.astype(jnp.float32) / LANES)

    def make_heat(i, carry):
        s = i // STEPS
        n = lax.rem(i, STEPS)
        row = index_smem[s]
        y0 = track_smem[n, row].astype(jnp.float32)
        level = power_smem[n, row].astype(jnp.float32)
        plane = prof_z * (DT * 0.5 * (1.0 + level))

        def rows(y, c):
            offset = ((sub * inner + y).astype(jnp.float32) - y0) * (16.0 / (inner * BLOCKS))
            heat[i, y] = plane * jnp.exp(-(offset * offset))
            return c

        return lax.fori_loop(0, inner, rows, carry, unroll=8)

    lax.fori_loop(0, 2 * STEPS, make_heat, 0)

    def clear(y, c):
        for p in range(planes):
            acc[p, y] = jnp.zeros((BLOCKS, LANES), jnp.float32)
        return c

    lax.fori_loop(0, inner, clear, 0)

    pl.semaphore_wait(barrier, jnp.where(has_far, 5, 4))

    for which, go in ((0, lambda i: move_temp(i, 0, 0)), (1, move_kap), (2, lambda i: move_temp(i, 1, 0))):
        for copy in loads[which]:
            copy.wait()
        for i in range(3):
            each_way(i, lambda go=go, i=i: go(i).start())

    def scale(p):
        for k in range(inner):
            kap[p, k] = HALF * kap[p, k]

    for i in range(3):
        each_way(i, lambda i=i: move_kap(i).wait_send())

    def scale_all(p, c):
        scale(p)
        return c

    lax.fori_loop(1, planes + 1, scale_all, 0)

    def wrapped(value, shift, last):
        return jnp.where(sub == last, 0.0, pltpu.roll(value, shift, 0))

    def across(ref, p, k):
        if k < 0:
            return wrapped(ref[p, inner - 1], 1, 0)
        if k == inner:
            return wrapped(ref[p, 0], BLOCKS - 1, BLOCKS - 1)
        return ref[p, k]

    def shifted(value):
        return pltpu.roll(value, LANES - 1, 1)

    def spread_temp(s, n):
        u_ref, a_ref = temp[n][s], coef[n][s]

        def first(p, k):
            roll_u[k] = shifted(u_ref[p, k])
            roll_a[k] = shifted(a_ref[p, k])

        def second(p, k):
            u, a = u_ref[p, k], a_ref[p, k]
            face = a + jnp.where(not_last, roll_a[k], 0.0)
            diff = jnp.where(not_last, roll_u[k], 0.0) - u
            g = face * diff
            az[n][s][p - 1, k] = face
            dz[n][s][p - 1, k] = diff
            hz[s][p - 1, k] = g
            hz_low[s][p - 1, k] = pltpu.roll(g, 1, 1)

        return first, second

    def spread_lam(s, n, whole):
        v_ref = lam[(n + 1) % 2][s]

        def first(p, k):
            roll_u[k] = shifted(v_ref[p, k])

        def second(p, k):
            d = jnp.where(not_last, roll_u[k], 0.0) - v_ref[p, k]
            m = dz[n][s][p - 1, k] * d
            mz[s][p - 1, k] = m
            mz_low[s][p - 1, k] = pltpu.roll(m, 1, 1)
            if whole:
                h = az[n][s][p - 1, k] * d
                hz[s][p - 1, k] = h
                hz_low[s][p - 1, k] = pltpu.roll(h, 1, 1)

        return first, second

    def plane_coef(s, n, p, rows=range(inner)):
        for k in rows:
            u = temp[n][s][p, k]
            coef[n][s][p, k] = kap[p, k] * recip(1.0 + u * u)

    def forward(s, n):
        u_ref, a_ref, new = temp[n][s], coef[n][s], temp[n + 1][s]

        def do(p, rows=range(inner)):
            u, a = u_ref[p, rows[0]], a_ref[p, rows[0]]
            low = (across(a_ref, p, rows[0] - 1) + a) * (u - across(u_ref, p, rows[0] - 1))
            for k in rows:
                uy, ay = across(u_ref, p, k + 1), across(a_ref, p, k + 1)
                high = (a + ay) * (uy - u)
                flux = (a + a_ref[p + 1, k]) * (u_ref[p + 1, k] - u)
                flux = flux + (a + a_ref[p - 1, k]) * (u_ref[p - 1, k] - u)
                flux = flux + (high - low)
                flux = flux + (hz[s][p - 1, k] - jnp.where(first_lane, a * u, hz_low[s][p - 1, k]))
                later = (u + heat[s * STEPS + n, k]) + flux
                new[p, k] = later
                if n + 1 < STEPS:
                    coef[n + 1][s][p, k] = kap[p, k] * recip(1.0 + later * later)
                low, u, a = high, uy, ay

        return do

    def backward(s, n):
        whole = n > 0
        u_ref, a_ref = temp[n][s], coef[n][s]
        v_ref, new = lam[(n + 1) % 2][s], lam[n % 2][s]

        def do(p, rows=range(inner)):
            u, v = u_ref[p, rows[0]], v_ref[p, rows[0]]
            d = v - across(v_ref, p, rows[0] - 1)
            m_low = (u - across(u_ref, p, rows[0] - 1)) * d
            if whole:
                a = a_ref[p, rows[0]]
                h_low = (a + across(a_ref, p, rows[0] - 1)) * d
            for k in rows:
                uy, vy = across(u_ref, p, k + 1), across(v_ref, p, k + 1)
                d = vy - v
                d_up, d_down = v_ref[p + 1, k] - v, v_ref[p - 1, k] - v
                m_high = (uy - u) * d
                total = (u_ref[p + 1, k] - u) * d_up + (u_ref[p - 1, k] - u) * d_down
                total = total + (m_high + m_low)
                total = total + (mz[s][p - 1, k] + jnp.where(first_lane, u * v, mz_low[s][p - 1, k]))
                t = total * recip(1.0 + u * u)
                acc[p - 1, k] = acc[p - 1, k] + t
                if whole:
                    ay = across(a_ref, p, k + 1)
                    h_high = (a + ay) * d
                    flux = (a + a_ref[p + 1, k]) * d_up + (a + a_ref[p - 1, k]) * d_down
                    flux = flux + (h_high - h_low)
                    flux = flux + (hz[s][p - 1, k] - jnp.where(first_lane, a * v, hz_low[s][p - 1, k]))
                    half = (a * u) * t
                    new[p, k] = (v + flux) + (half + half)
                    a, h_low = ay, h_high
                u, v, m_low = uy, vy, m_high

        return do

    def plane_of(t):
        away = jnp.where(top, t, planes + 1 - t)
        return jnp.where(t == 0, edge[0], away)

    def sweep(main, other, ahead, behind, at):
        for h in range(2):
            rows = range(h * part, (h + 1) * part)
            ahead(h)
            for k in rows:
                other[0](edge[0], k)
            main(edge[0], rows)
            behind(h)

        def body(t, c):
            for when, do in at.items():
                pl.when(t == when)(do)
            for one, q in ((other[1], plane_of(t - 1)), (other[0], plane_of(t))):
                for k in range(inner):
                    one(q, k)
            main(plane_of(t))
            return c

        lax.fori_loop(1, planes, body, 0)
        for k in range(inner):
            other[1](plane_of(planes - 1), k)

    def first_coef(p, c):
        for s in range(2):
            plane_coef(s, 0, p)
        return c

    lax.fori_loop(1, planes + 1, first_coef, 0)
    begin = spread_temp(0, 0)

    def begin_z(t, c):
        for one, q in ((begin[1], jnp.maximum(t, 1)), (begin[0], t + 1)):
            for k in range(inner):
                one(q, k)
        return c

    lax.fori_loop(0, planes, begin_z, 0)
    for k in range(inner):
        begin[1](planes, k)
    for i in range(3):
        each_way(i, lambda i=i: move_kap(i).wait_recv())
    for side in range(2):
        scale(halo[side])

    for n in range(STEPS):
        for s in range(2):

            def ahead(h, s=s, n=n):
                each_way(0, lambda: move_temp(h, s, n).wait_recv())
                plane_coef(s, n, halo[0], range(h * part, (h + 1) * part))

            def behind(h, s=s, n=n):
                if n + 1 < STEPS:
                    each_way(h, lambda: move_temp(h, s, n + 1).start())

            def near(s=s, n=n):
                move_temp(2, s, n).wait_recv()
                plane_coef(s, n, halo[1])

            at = {1: near}
            if n + 1 < STEPS:
                at[2] = lambda s=s, n=n: move_temp(2, s, n + 1).start()
            if s == 0:
                other = spread_temp(1, n)
            elif n + 1 < STEPS:
                other = spread_temp(0, n + 1)
            else:
                other = spread_lam(0, n, True)
            sweep(forward(s, n), other, ahead, behind, at)
        if n == STEPS - 2:
            for s in range(2):
                for copy in loads[3 + s]:
                    copy.wait()
                for i in range(3):
                    each_way(i, lambda i=i: move_lam(i, s, STEPS).start())

    stores = []
    for s in range(2):
        for b in range(BLOCKS):
            copy = pltpu.make_async_copy(
                temp[STEPS][s].at[pl.ds(1, planes), :, b, :],
                final_hbm.at[s, :, pl.ds(b * inner, inner), :],
                out_sem.at[s, b],
            )
            copy.start()
            stores.append(copy)

    for n in reversed(range(STEPS)):
        for s in range(2 if n > 0 else 1):

            def ahead(h, s=s, n=n):
                each_way(h, lambda: move_lam(h, s, n + 1).wait_recv())
                if h == 0 and 0 < n <= STEPS - 2:
                    for i in range(3):
                        each_way(i, lambda i=i: move_lam(i, s, n + 2).wait_send())

            def behind(h, s=s, n=n):
                if n > 0:
                    each_way(h, lambda: move_lam(h, s, n).start())

            at = {1: lambda s=s, n=n: move_lam(2, s, n + 1).wait_recv()}
            if n > 0:
                at[2] = lambda s=s, n=n: move_lam(2, s, n).start()
            if s == 0:
                other = spread_lam(1, n, n > 0)
            else:
                other = spread_lam(0, n - 1, n > 1)
            sweep(backward(s, n), other, ahead, behind, at)

    def row_of(t):
        return plane_of(t + 1) - 1

    def shares(t):
        q = row_of(t)
        return [
            pltpu.make_async_copy(acc.at[q, :, b, :], share.at[b // 4, b % 4, q], g_sem.at[t, b])
            for b in range(BLOCKS)
        ]

    def along_x(t, slot):
        right = (lax.rem(t, 2) == 0) if slot != 1 else (lax.rem(t, 2) == 1)
        column = x_far if slot == 0 else jnp.where(right, x_right, x_left)
        return pltpu.make_async_remote_copy(
            src_ref=share.at[:, column, row_of(t)],
            dst_ref=inbox.at[slot, t],
            send_sem=x_send.at[slot, t],
            recv_sem=x_recv.at[slot, t],
            device_id=(space, jnp.where(right, set_right, set_left)),
            device_id_type=MESH,
        )

    def along_y(t):
        q = row_of(t)
        return pltpu.make_async_remote_copy(
            src_ref=share.at[1 - own_y, own_x, q],
            dst_ref=inbox_y.at[q],
            send_sem=y_send.at[t],
            recv_sem=y_recv.at[t],
            device_id=(space, set_y),
            device_id_type=MESH,
        )

    def start_shares(t):
        for copy in shares(t):
            copy.start()

    def send_shares(t):
        for copy in shares(t):
            copy.wait()
        along_x(t, 0).start()

    def last_body(t, c):
        @pl.when(t == 0)
        def _():
            move_lam(2, 1, 1).wait_recv()

        @pl.when(t == planes - 1)
        def _():
            for h in range(2):
                each_way(h, lambda h=h: move_lam(h, 1, 1).wait_recv())

        pl.when(t >= 1)(lambda: start_shares(t - 1))
        pl.when(t >= 2)(lambda: send_shares(t - 2))
        backward(1, 0)(plane_of(t + 1))
        return c

    lax.fori_loop(0, planes, last_body, 0)
    start_shares(planes - 1)
    send_shares(planes - 2)
    send_shares(planes - 1)

    def pass_on(t, c):
        along_x(t, 0).wait_recv()
        q = row_of(t)
        column = jnp.where(lax.rem(t, 2) == 0, x_right, x_left)
        for y in range(2):
            share[y, column, q] = share[y, column, q] + inbox[0, t, y]
        along_x(t, 2).start()
        along_x(t, 1).start()
        return c

    lax.fori_loop(0, planes, pass_on, 0)

    def across_y(t, c):
        along_x(t, 1).wait_recv()
        along_x(t, 2).wait_recv()
        q = row_of(t)
        for y in (1 - own_y, own_y):
            share[y, own_x, q] = share[y, own_x, q] + (inbox[1, t, y] + inbox[2, t, y])
        along_y(t).start()
        return c

    lax.fori_loop(0, planes, across_y, 0)

    def give(t):
        q = row_of(t)
        return pltpu.make_async_copy(inbox_y.at[q], grad_hbm.at[q], out_sem.at[2, t])

    def last_add(t, c):
        along_y(t).wait_recv()
        q = row_of(t)
        inbox_y[q] = -HALF * (share[own_y, own_x, q] + inbox_y[q])
        give(t).start()
        return c

    lax.fori_loop(0, planes, last_add, 0)

    def drain(t, c):
        for slot in range(3):
            along_x(t, slot).wait_send()
        along_y(t).wait_send()
        give(t).wait()
        return c

    lax.fori_loop(0, planes, drain, 0)
    for s in range(2):
        for i in range(3):
            for n in range(STEPS):
                each_way(i, lambda s=s, i=i, n=n: move_temp(i, s, n).wait_send())
            for m in (1, 2):
                each_way(i, lambda s=s, i=i, m=m: move_lam(i, s, m).wait_send())
    for copy in stores:
        copy.wait()


def hand_over(final, gradient, final_out, gradient_out, held, held_grad, sems):
    spots = [(s, p) for s in range(final.shape[0]) for p in range(final.shape[1])]
    moves = [(gradient, held_grad, gradient_out)]
    moves += [(final.at[s, p], held.at[s, p], final_out.at[s, p]) for s, p in spots]
    loads = [pltpu.make_async_copy(a, b, sems.at[0, i]) for i, (a, b, _) in enumerate(moves)]
    stores = [pltpu.make_async_copy(b, c, sems.at[1, i]) for i, (_, b, c) in enumerate(moves)]
    for copy in loads:
        copy.start()
    for load, store in zip(loads, stores):
        load.wait()
        store.start()
    for store in stores:
        store.wait()


def local(set_size, space_size, initial, conductivity, weights, setting_index, track, power):
    settings, planes, y_count, lanes = initial.shape
    inner = y_count // BLOCKS
    tile = (inner, BLOCKS, lanes)
    any_ref = pl.BlockSpec(memory_space=pl.ANY)
    smem = pl.BlockSpec(memory_space=pltpu.SMEM)
    f32 = jnp.float32
    dma = pltpu.SemaphoreType.DMA
    final, gradient = pl.pallas_call(
        functools.partial(kernel, planes, inner, set_size, space_size),
        out_shape=(
            jax.ShapeDtypeStruct(initial.shape, f32),
            jax.ShapeDtypeStruct((planes, y_count // set_size, lanes), f32),
        ),
        in_specs=[any_ref] * 3 + [smem] * 3,
        out_specs=[any_ref] * 2,
        scratch_shapes=[pltpu.VMEM((planes + 2,) + tile, f32)] * (4 * STEPS + 2)
        + [pltpu.VMEM((planes,) + tile, f32)] * (4 * STEPS)
        + [pltpu.VMEM((planes + 2,) + tile, f32)] * 4
        + [pltpu.VMEM((planes,) + tile, f32)] * 8
        + [
            pltpu.VMEM((planes + 2,) + tile, f32),
            pltpu.VMEM((settings * STEPS,) + tile, f32),
            pltpu.VMEM((planes,) + tile, f32),
            pltpu.VMEM(tile, f32),
            pltpu.VMEM(tile, f32),
            pltpu.VMEM((2, 4, planes, inner, lanes), f32),
            pltpu.VMEM((3, planes, 2, inner, lanes), f32),
            pltpu.VMEM((planes, inner, lanes), f32),
            dma((5, BLOCKS)),
            dma((3, BLOCKS)),
            dma((3,)),
            dma((3,)),
            dma((3, settings, STEPS)),
            dma((3, settings, STEPS)),
            dma((3, settings, STEPS + 1)),
            dma((3, settings, STEPS + 1)),
            dma((planes, BLOCKS)),
            dma((3, planes)),
            dma((3, planes)),
            dma((planes,)),
            dma((planes,)),
        ],
        compiler_params=pltpu.CompilerParams(
            collective_id=0, has_side_effects=True, vmem_limit_bytes=62 * 2**20
        ),
    )(initial, conductivity, weights, setting_index, track.T, power.T)
    return pl.pallas_call(
        hand_over,
        out_shape=(
            jax.ShapeDtypeStruct(final.shape, f32),
            jax.ShapeDtypeStruct(gradient.shape, f32),
        ),
        in_specs=[any_ref] * 2,
        out_specs=[any_ref] * 2,
        scratch_shapes=[
            pltpu.VMEM(final.shape, f32),
            pltpu.VMEM(gradient.shape, f32),
            dma((2, settings * planes + 1)),
        ],
    )(final, gradient)


def solution(mesh):
    in_specs = (
        P("set", "space", None, None),
        P("space", None, None),
        P("set", "space", None, None),
        P("set"),
        P(),
        P(),
    )
    out_specs = (P("set", "space", None, None), P("space", "set", None))
    return jax.shard_map(
        functools.partial(local, mesh.shape["set"], mesh.shape["space"]),
        mesh=mesh,
        in_specs=in_specs,
        out_specs=out_specs,
        check_vma=False,
    )
```

```python
import functools

import jax
import jax.numpy as jnp
from jax import lax
from jax.experimental import pallas as pl
from jax.experimental.pallas import tpu as pltpu
from jax.sharding import PartitionSpec as P

STEPS = 4
DT = 0.15
HALF = 0.5 * DT
BLOCKS = 8
LANES = 128
MESH = pl.DeviceIdType.MESH


def recip(value):
    return pl.reciprocal(value, approx=True)


def kernel(planes, inner, set_size, space_size, *refs):
    init_hbm, cond_hbm, weights_hbm, index_smem, track_smem, power_smem, final_hbm, grad_hbm = refs[:8]
    refs = list(refs[8:])

    def take(*shape):
        if not shape:
            return refs.pop(0)
        return [take(*shape[1:]) for _ in range(shape[0])]

    temp = take(STEPS + 1, 2)
    coef = take(STEPS, 2)
    az = take(STEPS, 2)
    dz = take(STEPS, 2)
    lam = take(2, 2)
    hz, hz_low, mz, mz_low = (take(2) for _ in range(4))
    kap, heat, acc, roll_u, roll_a = (take() for _ in range(5))
    share, inbox, inbox_y = (take() for _ in range(3))
    in_sem, out_sem, k_send, k_recv, u_send, u_recv, l_send, l_recv, g_sem, x_send, x_recv, y_send, y_recv = (
        take() for _ in range(13)
    )
    space = lax.axis_index("space")
    own_set = lax.axis_index("set")
    core = lax.rem(space, 2)
    top = core == 1
    edge = (jnp.where(top, planes, 1), jnp.where(top, 1, planes))
    halo = (jnp.where(top, planes + 1, 0), jnp.where(top, 0, planes + 1))
    there = (jnp.where(top, 0, planes + 1), jnp.where(top, planes + 1, 0))
    partner = (
        jnp.clip(jnp.where(top, space + 1, space - 1), 0, space_size - 1),
        jnp.where(top, space - 1, space + 1),
    )
    has_far = jnp.logical_and(space != 0, space != space_size - 1)
    lane = lax.broadcasted_iota(jnp.int32, (BLOCKS, LANES), 1)
    sub = lax.broadcasted_iota(jnp.int32, (BLOCKS, LANES), 0)
    not_last = lane < LANES - 1
    first_lane = lane == 0

    def relayout(src, dst, sem):
        return [
            pltpu.make_async_copy(
                src.at[:, pl.ds(b * inner, inner), :],
                dst.at[pl.ds(1, planes), :, b, :],
                sem.at[b],
            )
            for b in range(BLOCKS)
        ]

    loads = [
        relayout(init_hbm.at[0], temp[0][0], in_sem.at[0]),
        relayout(cond_hbm, kap, in_sem.at[1]),
        relayout(init_hbm.at[1], temp[0][1], in_sem.at[2]),
        relayout(weights_hbm.at[0], lam[0][0], in_sem.at[3]),
        relayout(weights_hbm.at[1], lam[0][1], in_sem.at[4]),
    ]
    for group in loads:
        for copy in group:
            copy.start()

    barrier = pltpu.get_barrier_semaphore()
    pl.semaphore_signal(barrier, inc=1, device_id=(partner[1], own_set), device_id_type=MESH)

    @pl.when(has_far)
    def _():
        pl.semaphore_signal(barrier, inc=1, device_id=(partner[0], own_set), device_id_type=MESH)

    own_y, own_x = own_set // 4, lax.rem(own_set, 4)
    x_right, x_left, x_far = (lax.rem(own_x + i, 4) for i in (1, 3, 2))
    set_right, set_left = own_y * 4 + x_right, own_y * 4 + x_left
    set_y = (1 - own_y) * 4 + own_x
    for other_set in (set_right, set_left, set_y):
        pl.semaphore_signal(barrier, inc=1, device_id=(space, other_set), device_id_type=MESH)

    part = inner // 2

    def swap(ref, lane_id, send, recv):
        side = lane_id // 2
        rows = pl.ds(0, inner) if side else pl.ds(lane_id * part, part)
        return pltpu.make_async_remote_copy(
            src_ref=ref.at[edge[side], rows],
            dst_ref=ref.at[there[side], rows],
            send_sem=send,
            recv_sem=recv,
            device_id=(partner[side], own_set),
            device_id_type=MESH,
        )

    def move_temp(i, s, n):
        return swap(temp[n][s], i, u_send.at[i, s, n], u_recv.at[i, s, n])

    def move_lam(i, s, m):
        return swap(lam[m % 2][s], i, l_send.at[i, s, m], l_recv.at[i, s, m])

    def move_kap(i):
        return swap(kap, i, k_send.at[i], k_recv.at[i])

    def each_way(i, do):
        if i == 2:
            do()
        else:
            pl.when(has_far)(do)

    @pl.when(jnp.logical_not(has_far))
    def _():
        zero = jnp.zeros((inner, BLOCKS, LANES), jnp.float32)
        kap[halo[0]] = zero
        for s in range(2):
            for n in range(STEPS):
                temp[n][s][halo[0]] = zero
            for n in range(2):
                lam[n][s][halo[0]] = zero

    pl.semaphore_wait(barrier, jnp.where(has_far, 5, 4))

    for which, go in ((0, lambda i: move_temp(i, 0, 0)), (1, move_kap), (2, lambda i: move_temp(i, 1, 0))):
        for copy in loads[which]:
            copy.wait()
        for i in range(3):
            each_way(i, lambda go=go, i=i: go(i).start())

    def scale(p):
        for k in range(inner):
            kap[p, k] = HALF * kap[p, k]

    prof_z = jnp.exp(-4.0 * lane.astype(jnp.float32) / LANES)

    def make_heat(i, carry):
        s = i // STEPS
        n = lax.rem(i, STEPS)
        row = index_smem[s]
        y0 = track_smem[n, row].astype(jnp.float32)
        level = power_smem[n, row].astype(jnp.float32)
        plane = prof_z * (DT * 0.5 * (1.0 + level))

        def rows(y, c):
            offset = ((sub * inner + y).astype(jnp.float32) - y0) * (16.0 / (inner * BLOCKS))
            heat[i, y] = plane * jnp.exp(-(offset * offset))
            return c

        return lax.fori_loop(0, inner, rows, carry, unroll=8)

    lax.fori_loop(0, 2 * STEPS, make_heat, 0)

    def clear(y, c):
        for p in range(planes):
            acc[p, y] = jnp.zeros((BLOCKS, LANES), jnp.float32)
        return c

    lax.fori_loop(0, inner, clear, 0)

    for i in range(3):
        each_way(i, lambda i=i: move_kap(i).wait_send())

    def scale_all(p, c):
        scale(p)
        return c

    lax.fori_loop(1, planes + 1, scale_all, 0)

    def wrapped(value, shift, last):
        return jnp.where(sub == last, 0.0, pltpu.roll(value, shift, 0))

    def across(ref, p, k):
        if k < 0:
            return wrapped(ref[p, inner - 1], 1, 0)
        if k == inner:
            return wrapped(ref[p, 0], BLOCKS - 1, BLOCKS - 1)
        return ref[p, k]

    def shifted(value):
        return pltpu.roll(value, LANES - 1, 1)

    def spread_temp(s, n):
        u_ref, a_ref = temp[n][s], coef[n][s]

        def first(p, k):
            roll_u[k] = shifted(u_ref[p, k])
            roll_a[k] = shifted(a_ref[p, k])

        def second(p, k):
            u, a = u_ref[p, k], a_ref[p, k]
            face = a + jnp.where(not_last, roll_a[k], 0.0)
            diff = jnp.where(not_last, roll_u[k], 0.0) - u
            g = face * diff
            az[n][s][p - 1, k] = face
            dz[n][s][p - 1, k] = diff
            hz[s][p - 1, k] = g
            hz_low[s][p - 1, k] = pltpu.roll(g, 1, 1)

        return first, second

    def spread_lam(s, n, whole):
        v_ref = lam[(n + 1) % 2][s]

        def first(p, k):
            roll_u[k] = shifted(v_ref[p, k])

        def second(p, k):
            d = jnp.where(not_last, roll_u[k], 0.0) - v_ref[p, k]
            m = dz[n][s][p - 1, k] * d
            mz[s][p - 1, k] = m
            mz_low[s][p - 1, k] = pltpu.roll(m, 1, 1)
            if whole:
                h = az[n][s][p - 1, k] * d
                hz[s][p - 1, k] = h
                hz_low[s][p - 1, k] = pltpu.roll(h, 1, 1)

        return first, second

    def plane_coef(s, n, p, rows=range(inner)):
        for k in rows:
            u = temp[n][s][p, k]
            coef[n][s][p, k] = kap[p, k] * recip(1.0 + u * u)

    def forward(s, n):
        u_ref, a_ref, new = temp[n][s], coef[n][s], temp[n + 1][s]

        def do(p, rows=range(inner)):
            u, a = u_ref[p, rows[0]], a_ref[p, rows[0]]
            low = (across(a_ref, p, rows[0] - 1) + a) * (u - across(u_ref, p, rows[0] - 1))
            for k in rows:
                uy, ay = across(u_ref, p, k + 1), across(a_ref, p, k + 1)
                high = (a + ay) * (uy - u)
                flux = (a + a_ref[p + 1, k]) * (u_ref[p + 1, k] - u)
                flux = flux + (a + a_ref[p - 1, k]) * (u_ref[p - 1, k] - u)
                flux = flux + (high - low)
                flux = flux + (hz[s][p - 1, k] - jnp.where(first_lane, a * u, hz_low[s][p - 1, k]))
                later = (u + heat[s * STEPS + n, k]) + flux
                new[p, k] = later
                if n + 1 < STEPS:
                    coef[n + 1][s][p, k] = kap[p, k] * recip(1.0 + later * later)
                low, u, a = high, uy, ay

        return do

    def backward(s, n):
        whole = n > 0
        u_ref, a_ref = temp[n][s], coef[n][s]
        v_ref, new = lam[(n + 1) % 2][s], lam[n % 2][s]

        def do(p, rows=range(inner)):
            u, v = u_ref[p, rows[0]], v_ref[p, rows[0]]
            d = v - across(v_ref, p, rows[0] - 1)
            m_low = (u - across(u_ref, p, rows[0] - 1)) * d
            if whole:
                a = a_ref[p, rows[0]]
                h_low = (a + across(a_ref, p, rows[0] - 1)) * d
            for k in rows:
                uy, vy = across(u_ref, p, k + 1), across(v_ref, p, k + 1)
                d = vy - v
                d_up, d_down = v_ref[p + 1, k] - v, v_ref[p - 1, k] - v
                m_high = (uy - u) * d
                total = (u_ref[p + 1, k] - u) * d_up + (u_ref[p - 1, k] - u) * d_down
                total = total + (m_high + m_low)
                total = total + (mz[s][p - 1, k] + jnp.where(first_lane, u * v, mz_low[s][p - 1, k]))
                t = total * recip(1.0 + u * u)
                acc[p - 1, k] = acc[p - 1, k] + t
                if whole:
                    ay = across(a_ref, p, k + 1)
                    h_high = (a + ay) * d
                    flux = (a + a_ref[p + 1, k]) * d_up + (a + a_ref[p - 1, k]) * d_down
                    flux = flux + (h_high - h_low)
                    flux = flux + (hz[s][p - 1, k] - jnp.where(first_lane, a * v, hz_low[s][p - 1, k]))
                    half = (a * u) * t
                    new[p, k] = (v + flux) + (half + half)
                    a, h_low = ay, h_high
                u, v, m_low = uy, vy, m_high

        return do

    def plane_of(t):
        away = jnp.where(top, t, planes + 1 - t)
        return jnp.where(t == 0, edge[0], away)

    def sweep(main, other, ahead, behind, at):
        for h in range(2):
            rows = range(h * part, (h + 1) * part)
            ahead(h)
            for k in rows:
                other[0](edge[0], k)
            main(edge[0], rows)
            behind(h)

        def body(t, c):
            for when, do in at.items():
                pl.when(t == when)(do)
            for one, q in ((other[1], plane_of(t - 1)), (other[0], plane_of(t))):
                for k in range(inner):
                    one(q, k)
            main(plane_of(t))
            return c

        lax.fori_loop(1, planes, body, 0)
        for k in range(inner):
            other[1](plane_of(planes - 1), k)

    def first_coef(p, c):
        for s in range(2):
            plane_coef(s, 0, p)
        return c

    lax.fori_loop(1, planes + 1, first_coef, 0)
    begin = spread_temp(0, 0)

    def begin_z(t, c):
        for one, q in ((begin[1], jnp.maximum(t, 1)), (begin[0], t + 1)):
            for k in range(inner):
                one(q, k)
        return c

    lax.fori_loop(0, planes, begin_z, 0)
    for k in range(inner):
        begin[1](planes, k)
    for i in range(3):
        each_way(i, lambda i=i: move_kap(i).wait_recv())
    for side in range(2):
        scale(halo[side])

    for n in range(STEPS):
        for s in range(2):

            def ahead(h, s=s, n=n):
                each_way(0, lambda: move_temp(h, s, n).wait_recv())
                plane_coef(s, n, halo[0], range(h * part, (h + 1) * part))

            def behind(h, s=s, n=n):
                if n + 1 < STEPS:
                    each_way(h, lambda: move_temp(h, s, n + 1).start())

            def near(s=s, n=n):
                move_temp(2, s, n).wait_recv()
                plane_coef(s, n, halo[1])

            at = {1: near}
            if n + 1 < STEPS:
                at[2] = lambda s=s, n=n: move_temp(2, s, n + 1).start()
            if s == 0:
                other = spread_temp(1, n)
            elif n + 1 < STEPS:
                other = spread_temp(0, n + 1)
            else:
                other = spread_lam(0, n, True)
            sweep(forward(s, n), other, ahead, behind, at)
        if n == STEPS - 2:
            for s in range(2):
                for copy in loads[3 + s]:
                    copy.wait()
                for i in range(3):
                    each_way(i, lambda i=i: move_lam(i, s, STEPS).start())

    stores = []
    for s in range(2):
        for b in range(BLOCKS):
            copy = pltpu.make_async_copy(
                temp[STEPS][s].at[pl.ds(1, planes), :, b, :],
                final_hbm.at[s, :, pl.ds(b * inner, inner), :],
                out_sem.at[s, b],
            )
            copy.start()
            stores.append(copy)

    for n in reversed(range(STEPS)):
        for s in range(2 if n > 0 else 1):

            def ahead(h, s=s, n=n):
                each_way(h, lambda: move_lam(h, s, n + 1).wait_recv())
                if h == 0 and 0 < n <= STEPS - 2:
                    for i in range(3):
                        each_way(i, lambda i=i: move_lam(i, s, n + 2).wait_send())

            def behind(h, s=s, n=n):
                if n > 0:
                    each_way(h, lambda: move_lam(h, s, n).start())

            at = {1: lambda s=s, n=n: move_lam(2, s, n + 1).wait_recv()}
            if n > 0:
                at[2] = lambda s=s, n=n: move_lam(2, s, n).start()
            if s == 0:
                other = spread_lam(1, n, n > 0)
            else:
                other = spread_lam(0, n - 1, n > 1)
            sweep(backward(s, n), other, ahead, behind, at)

    def row_of(t):
        return plane_of(t + 1) - 1

    def shares(t):
        q = row_of(t)
        return [
            pltpu.make_async_copy(acc.at[q, :, b, :], share.at[b // 4, b % 4, q], g_sem.at[t, b])
            for b in range(BLOCKS)
        ]

    def along_x(t, slot):
        right = (lax.rem(t, 2) == 0) if slot != 1 else (lax.rem(t, 2) == 1)
        column = x_far if slot == 0 else jnp.where(right, x_right, x_left)
        return pltpu.make_async_remote_copy(
            src_ref=share.at[:, column, row_of(t)],
            dst_ref=inbox.at[slot, t],
            send_sem=x_send.at[slot, t],
            recv_sem=x_recv.at[slot, t],
            device_id=(space, jnp.where(right, set_right, set_left)),
            device_id_type=MESH,
        )

    def along_y(t):
        q = row_of(t)
        return pltpu.make_async_remote_copy(
            src_ref=share.at[1 - own_y, own_x, q],
            dst_ref=inbox_y.at[q],
            send_sem=y_send.at[t],
            recv_sem=y_recv.at[t],
            device_id=(space, set_y),
            device_id_type=MESH,
        )

    def start_shares(t):
        for copy in shares(t):
            copy.start()

    def send_shares(t):
        for copy in shares(t):
            copy.wait()
        along_x(t, 0).start()

    def last_body(t, c):
        @pl.when(t == 0)
        def _():
            move_lam(2, 1, 1).wait_recv()

        @pl.when(t == planes - 1)
        def _():
            for h in range(2):
                each_way(h, lambda h=h: move_lam(h, 1, 1).wait_recv())

        pl.when(t >= 1)(lambda: start_shares(t - 1))
        pl.when(t >= 2)(lambda: send_shares(t - 2))
        backward(1, 0)(plane_of(t + 1))
        return c

    lax.fori_loop(0, planes, last_body, 0)
    start_shares(planes - 1)
    send_shares(planes - 2)
    send_shares(planes - 1)

    def pass_on(t, c):
        along_x(t, 0).wait_recv()
        q = row_of(t)
        column = jnp.where(lax.rem(t, 2) == 0, x_right, x_left)
        for y in range(2):
            share[y, column, q] = share[y, column, q] + inbox[0, t, y]
        along_x(t, 2).start()
        along_x(t, 1).start()
        return c

    lax.fori_loop(0, planes, pass_on, 0)

    def across_y(t, c):
        along_x(t, 1).wait_recv()
        along_x(t, 2).wait_recv()
        q = row_of(t)
        for y in (1 - own_y, own_y):
            share[y, own_x, q] = share[y, own_x, q] + (inbox[1, t, y] + inbox[2, t, y])
        along_y(t).start()
        return c

    lax.fori_loop(0, planes, across_y, 0)

    def give(t):
        q = row_of(t)
        return pltpu.make_async_copy(inbox_y.at[q], grad_hbm.at[q], out_sem.at[2, t])

    def last_add(t, c):
        along_y(t).wait_recv()
        q = row_of(t)
        inbox_y[q] = -HALF * (share[own_y, own_x, q] + inbox_y[q])
        give(t).start()
        return c

    lax.fori_loop(0, planes, last_add, 0)

    def drain(t, c):
        for slot in range(3):
            along_x(t, slot).wait_send()
        along_y(t).wait_send()
        give(t).wait()
        return c

    lax.fori_loop(0, planes, drain, 0)
    for s in range(2):
        for i in range(3):
            for n in range(STEPS):
                each_way(i, lambda s=s, i=i, n=n: move_temp(i, s, n).wait_send())
            for m in (1, 2):
                each_way(i, lambda s=s, i=i, m=m: move_lam(i, s, m).wait_send())
    for copy in stores:
        copy.wait()


def hand_over(final, gradient, final_out, gradient_out, held, held_grad, sems):
    spots = [(s, p) for s in range(final.shape[0]) for p in range(final.shape[1])]
    moves = [(gradient, held_grad, gradient_out)]
    moves += [(final.at[s, p], held.at[s, p], final_out.at[s, p]) for s, p in spots]
    loads = [pltpu.make_async_copy(a, b, sems.at[0, i]) for i, (a, b, _) in enumerate(moves)]
    stores = [pltpu.make_async_copy(b, c, sems.at[1, i]) for i, (_, b, c) in enumerate(moves)]
    for copy in loads:
        copy.start()
    for load, store in zip(loads, stores):
        load.wait()
        store.start()
    for store in stores:
        store.wait()


def local(set_size, space_size, initial, conductivity, weights, setting_index, track, power):
    settings, planes, y_count, lanes = initial.shape
    inner = y_count // BLOCKS
    tile = (inner, BLOCKS, lanes)
    any_ref = pl.BlockSpec(memory_space=pl.ANY)
    smem = pl.BlockSpec(memory_space=pltpu.SMEM)
    f32 = jnp.float32
    dma = pltpu.SemaphoreType.DMA
    final, gradient = pl.pallas_call(
        functools.partial(kernel, planes, inner, set_size, space_size),
        out_shape=(
            jax.ShapeDtypeStruct(initial.shape, f32),
            jax.ShapeDtypeStruct((planes, y_count // set_size, lanes), f32),
        ),
        in_specs=[any_ref] * 3 + [smem] * 3,
        out_specs=[any_ref] * 2,
        scratch_shapes=[pltpu.VMEM((planes + 2,) + tile, f32)] * (4 * STEPS + 2)
        + [pltpu.VMEM((planes,) + tile, f32)] * (4 * STEPS)
        + [pltpu.VMEM((planes + 2,) + tile, f32)] * 4
        + [pltpu.VMEM((planes,) + tile, f32)] * 8
        + [
            pltpu.VMEM((planes + 2,) + tile, f32),
            pltpu.VMEM((settings * STEPS,) + tile, f32),
            pltpu.VMEM((planes,) + tile, f32),
            pltpu.VMEM(tile, f32),
            pltpu.VMEM(tile, f32),
            pltpu.VMEM((2, 4, planes, inner, lanes), f32),
            pltpu.VMEM((3, planes, 2, inner, lanes), f32),
            pltpu.VMEM((planes, inner, lanes), f32),
            dma((5, BLOCKS)),
            dma((3, BLOCKS)),
            dma((3,)),
            dma((3,)),
            dma((3, settings, STEPS)),
            dma((3, settings, STEPS)),
            dma((3, settings, STEPS + 1)),
            dma((3, settings, STEPS + 1)),
            dma((planes, BLOCKS)),
            dma((3, planes)),
            dma((3, planes)),
            dma((planes,)),
            dma((planes,)),
        ],
        compiler_params=pltpu.CompilerParams(
            collective_id=0, has_side_effects=True, vmem_limit_bytes=62 * 2**20
        ),
    )(initial, conductivity, weights, setting_index, track.T, power.T)
    return pl.pallas_call(
        hand_over,
        out_shape=(
            jax.ShapeDtypeStruct(final.shape, f32),
            jax.ShapeDtypeStruct(gradient.shape, f32),
        ),
        in_specs=[any_ref] * 2,
        out_specs=[any_ref] * 2,
        scratch_shapes=[
            pltpu.VMEM(final.shape, f32),
            pltpu.VMEM(gradient.shape, f32),
            dma((2, settings * planes + 1)),
        ],
    )(final, gradient)


def solution(mesh):
    in_specs = (
        P("set", "space", None, None),
        P("space", None, None),
        P("set", "space", None, None),
        P("set"),
        P(),
        P(),
    )
    out_specs = (P("set", "space", None, None), P("space", "set", None))
    return jax.shard_map(
        functools.partial(local, mesh.shape["set"], mesh.shape["space"]),
        mesh=mesh,
        in_specs=in_specs,
        out_specs=out_specs,
        check_vma=False,
    )
```
